32 devices in a mesh: seq: 8 (over z, y), tp: 4 (over x, core).
Axes of the slice: x: 2, y: 2, z: 4, core: 2. Of those that a mesh axis runs over, the one named last changes fastest.
Arguments:
- tokens: bfloat16 [64, 1152], P('seq'), may hold values from -6 to 6
- attn_gain: float32 [1152], replicated, may hold values from 0.1 to 1.9
- w_query: bfloat16 [1152, 1280], P(None, 'tp'), may hold values from -0.1875 to 0.1875
- w_key: bfloat16 [1152, 384], replicated, may hold values from -0.1875 to 0.1875
- w_value: bfloat16 [1152, 384], replicated, may hold values from -0.1875 to 0.1875
- w_out: bfloat16 [1280, 1152], P('tp'), may hold values from -0.1875 to 0.1875
- prefix_keys: bfloat16 [8, 4096, 384], P(None, 'seq'), may hold values from -92 to 92
- prefix_values: bfloat16 [8, 4096, 384], P(None, 'seq'), may hold values from -6 to 6
- suffix_keys: bfloat16 [64, 128, 384], P('seq'), may hold values from -92 to 92
- suffix_values: bfloat16 [64, 128, 384], P('seq'), may hold values from -6 to 6
- group_of: int32 [64], replicated, may hold values from 0 to 7, as said below
- prefix_len: int32 [8], replicated, may hold values from 1 to 4096, as said below
- suffix_len: int32 [64], replicated, may hold values from 0 to 128, as said below
- mlp_gain: float32 [1152], replicated, may hold values from 0.1 to 1.9
- w_gate: bfloat16 [1152, 3072], P(None, 'tp'), may hold values from -0.1875 to 0.1875
- w_up: bfloat16 [1152, 3072], P(None, 'tp'), may hold values from -0.1875 to 0.1875
- w_down: bfloat16 [3072, 1152], P('tp'), may hold values from -0.109375 to 0.109375
Outputs:
- layer_out: bfloat16 [64, 1152], P('seq')
The draws below stay inside these ranges and needn't reach their ends.
Inputs may be any that keep to these rules, and one draw needn't show every extreme that they name: `group_of`: prompt group of each request; every request reads its group's stored prefix. `prefix_len`: stored prefix positions in use for each group. `suffix_len`: stored suffix positions in use for each request.
All inputs are finite; a program needn't handle non-finite values.
Results may differ from the reference program's by a relative error of at most 0.018.
Values may be sent and summed in bfloat16 or wider, within the bound.
A program may use at most 192 MiB of HBM per device.

```python
import jax
import jax.numpy as jnp
import numpy as np
from jax import lax

D = 1152
HEADS = 18
KV_HEADS = 6
HD = 64
FF = 3072
SLEN = 128
GROUPS = 8
SLOTS = 5
QCOLS = 1280
REQ = 64
PLEN = 4096
N_TP = 4


def pinned(base_key, item_count, lowest, highest):
    drawn = jax.random.randint(base_key, (item_count,), lowest, highest + 1, jnp.int32)
    chosen = jax.random.randint(jax.random.fold_in(base_key, 3), (), 0, item_count, jnp.int32)
    drawn = drawn.at[chosen].set(highest)
    return drawn.at[(chosen + 1) % item_count].set(lowest)


def draw_group_of(key, part):
    return pinned(key, REQ, 0, GROUPS - 1)


def draw_prefix_len(key, part):
    return pinned(key, GROUPS, 1, PLEN)


def draw_suffix_len(key, part):
    return pinned(key, REQ, 0, SLEN)


def draw_prefix_keys(key, part):
    shape_all = (GROUPS, PLEN, KV_HEADS * HD)
    return (3.0 * jnp.clip(jax.random.normal(key, shape_all, jnp.float32), -5.0, 5.0)).astype(jnp.bfloat16)


def draw_suffix_keys(key, part):
    shape_all = (REQ, SLEN, KV_HEADS * HD)
    return (3.0 * jnp.clip(jax.random.normal(key, shape_all, jnp.float32), -5.0, 5.0)).astype(jnp.bfloat16)


def steps_of(rng, dims, split, low, high):
    gain, own = 1.0, jax.random.fold_in(rng, 6)
    for dim, blocks in split:
        heights = jnp.exp(jax.random.uniform(jax.random.fold_in(own, dim), (blocks,), jnp.float32, low / len(split), high / len(split)))
        gain = gain * jnp.repeat(heights, dims[dim] // blocks).reshape([-1 if axis == dim else 1 for axis in range(len(dims))])
    return gain


def scatter_about(rng, extent, width, bound, shards=(), kind=jnp.bfloat16):
    level = steps_of(rng, extent, shards, -0.22, 0.18) if shards else 1.0
    values = jax.random.normal(rng, extent, jnp.float32) * width * level
    return jnp.minimum(jnp.maximum(values, -bound), bound).astype(kind)


def setup_inputs(seed: int = 0) -> dict:
    splits = jax.random.split(jax.random.key(seed), 18)
    tokens = scatter_about(splits[0], (REQ, D), 1.0, 6.0, ((0, 8),))
    attn_gain = jnp.clip(1.0 + 0.18 * jax.random.normal(splits[1], (D,), jnp.float32), 0.1, 1.9)
    w_query = scatter_about(splits[2], (D, QCOLS), D ** -0.5, 0.1875, ((1, 4),))
    w_key = scatter_about(splits[3], (D, KV_HEADS * HD), D ** -0.5, 0.1875)
    w_value = scatter_about(splits[4], (D, KV_HEADS * HD), D ** -0.5, 0.1875)
    w_out = scatter_about(splits[5], (QCOLS, D), (HEADS * HD) ** -0.5, 0.1875, ((0, 4),))
    prefix_keys = draw_prefix_keys(jax.random.fold_in(splits[17], 71), 0)
    prefix_values = scatter_about(splits[7], (GROUPS, PLEN, KV_HEADS * HD), 1.0, 6.0, ((1, 8),))
    suffix_keys = draw_suffix_keys(jax.random.fold_in(splits[17], 71), 0)
    suffix_values = scatter_about(splits[9], (REQ, SLEN, KV_HEADS * HD), 1.0, 6.0, ((0, 8),))
    group_of = draw_group_of(jax.random.fold_in(splits[17], 71), 0)
    prefix_len = draw_prefix_len(jax.random.fold_in(splits[17], 71), 0)
    suffix_len = draw_suffix_len(jax.random.fold_in(splits[17], 71), 0)
    mlp_gain = jnp.clip(1.0 + 0.18 * jax.random.normal(splits[13], (D,), jnp.float32), 0.1, 1.9)
    w_gate = scatter_about(splits[14], (D, FF), D ** -0.5, 0.1875, ((1, 4),))
    w_up = scatter_about(splits[15], (D, FF), D ** -0.5, 0.1875, ((1, 4),))
    w_down = scatter_about(splits[16], (FF, D), FF ** -0.5, 0.109375, ((0, 4),))
    return dict(tokens=tokens, attn_gain=attn_gain, w_query=w_query, w_key=w_key, w_value=w_value, w_out=w_out, prefix_keys=prefix_keys, prefix_values=prefix_values, suffix_keys=suffix_keys, suffix_values=suffix_values, group_of=group_of, prefix_len=prefix_len, suffix_len=suffix_len, mlp_gain=mlp_gain, w_gate=w_gate, w_up=w_up, w_down=w_down)


NEG_FILL = -1e+30

def rms_scale(values_in, gain_row):
    widened = values_in.astype(jnp.float32)
    factor = lax.rsqrt(lax.optimization_barrier(jnp.mean(widened * widened, axis=-1, keepdims=True)) + 1e-05)
    return (widened * factor * gain_row).astype(jnp.bfloat16)

def rotate_heads(blocks, position):
    half_dim = blocks.shape[-1] // 2
    frequency = jnp.power(10000.0, -jnp.arange(half_dim, dtype=jnp.float32) / half_dim)
    angles = position.astype(jnp.float32)[:, None, None] * frequency
    cosine = jnp.cos(angles)
    sine_part = jnp.sin(angles)
    low_half = blocks[..., :half_dim]
    high_half = blocks[..., half_dim:]
    return jnp.concatenate([low_half * cosine - high_half * sine_part, high_half * cosine + low_half * sine_part], axis=-1)

def slot_tables():
    per_device = HEADS // N_TP
    surplus = HEADS % N_TP
    slot_ids = np.arange(N_TP * SLOTS)
    device_ids = slot_ids // SLOTS
    within_ids = slot_ids % SLOTS
    head_ids = per_device * device_ids + np.minimum(device_ids, surplus) + within_ids
    slot_used = within_ids < per_device + (device_ids < surplus)
    kv_table = np.minimum(head_ids, HEADS - 1) // (HEADS // KV_HEADS)
    return (kv_table.astype(np.int32), slot_used.astype(np.float32))

def reference(tokens, attn_gain, w_query, w_key, w_value, w_out, prefix_keys, prefix_values, suffix_keys, suffix_values, group_of, prefix_len, suffix_len, mlp_gain, w_gate, w_up, w_down):
    kv_table, used_table = slot_tables()
    kv_ids = jnp.asarray(kv_table, jnp.int32)
    slot_used = jnp.asarray(used_table, jnp.float32)
    slot_total = kv_table.shape[0]
    normed = rms_scale(tokens, attn_gain)
    queries = jnp.dot(normed, w_query, preferred_element_type=jnp.float32).reshape(REQ, slot_total, HD)
    new_keys = jnp.dot(normed, w_key, preferred_element_type=jnp.float32).reshape(REQ, KV_HEADS, HD)
    new_values = jnp.dot(normed, w_value, preferred_element_type=jnp.float32).astype(jnp.bfloat16).reshape(REQ, KV_HEADS, HD)
    own_prefix = jnp.take(prefix_len, group_of)
    position = own_prefix + suffix_len
    queries = rotate_heads(queries, position).astype(jnp.bfloat16)
    new_keys = rotate_heads(new_keys, position).astype(jnp.bfloat16)
    score_scale = HD ** (-0.5)
    spots = jnp.arange(PLEN + SLEN, dtype=jnp.int32)

    def one_request(request_items):
        query_row, key_row, value_row, group_id, prefix_live, suffix_live, suffix_key_rows, suffix_value_rows = request_items
        prefix_key_rows = lax.dynamic_index_in_dim(prefix_keys, group_id, 0, keepdims=False)
        prefix_value_rows = lax.dynamic_index_in_dim(prefix_values, group_id, 0, keepdims=False)
        keys_all = jnp.concatenate([prefix_key_rows, suffix_key_rows], axis=0).reshape(-1, KV_HEADS, HD)
        values_all = jnp.concatenate([prefix_value_rows, suffix_value_rows], axis=0).reshape(-1, KV_HEADS, HD)
        keys_slot = jnp.take(keys_all, kv_ids, axis=1).astype(jnp.float32)
        values_slot = jnp.take(values_all, kv_ids, axis=1).astype(jnp.float32)
        query_wide = query_row.astype(jnp.float32)
        scores = jnp.einsum('sd,psd->sp', query_wide, keys_slot) * score_scale
        own_score = lax.optimization_barrier(jnp.sum(query_wide * jnp.take(key_row, kv_ids, axis=0).astype(jnp.float32), axis=-1)) * score_scale
        live = jnp.where(spots < PLEN, spots < prefix_live, spots - PLEN < suffix_live)
        top_score = jnp.maximum(lax.optimization_barrier(jnp.max(jnp.where(live[None, :], scores, NEG_FILL), axis=1)), own_score)
        weights = jnp.where(live[None, :], jnp.exp(scores - top_score[:, None]), 0.0)
        own_weight = jnp.exp(own_score - top_score)
        denominator = lax.optimization_barrier(jnp.sum(weights, axis=1)) + own_weight
        weights_low = lax.optimization_barrier(weights.astype(jnp.bfloat16)).astype(jnp.float32)
        own_low = lax.optimization_barrier(own_weight.astype(jnp.bfloat16)).astype(jnp.float32)
        numerator = jnp.einsum('sp,psd->sd', weights_low, values_slot)
        numerator = numerator + own_low[:, None] * jnp.take(value_row, kv_ids, axis=0).astype(jnp.float32)
        return (numerator / denominator[:, None] * slot_used[:, None]).astype(jnp.bfloat16)
    attended = lax.map(one_request, (queries, new_keys, new_values, group_of, own_prefix, suffix_len, suffix_keys, suffix_values))
    head_total = jnp.dot(attended.reshape(REQ, slot_total * HD), w_out, preferred_element_type=jnp.float32)
    hidden = (tokens.astype(jnp.float32) + head_total).astype(jnp.bfloat16)
    mlp_in = rms_scale(hidden, mlp_gain)
    gate_part = jnp.dot(mlp_in, w_gate, preferred_element_type=jnp.float32)
    up_part = jnp.dot(mlp_in, w_up, preferred_element_type=jnp.float32)
    activation = (jax.nn.silu(gate_part) * up_part).astype(jnp.bfloat16)
    down_total = jnp.dot(activation, w_down, preferred_element_type=jnp.float32)
    return (hidden.astype(jnp.float32) + down_total).astype(jnp.bfloat16)
```

```python
import functools

import jax
import jax.numpy as jnp
from jax import lax
from jax.experimental import pallas as pl
from jax.experimental.pallas import tpu as pltpu
from jax.sharding import PartitionSpec as P

HEADS = 18
KV_HEADS = 6
HD = 64
NEG = -1e30
WIDE = 256
PACK = 384
MESH = pl.DeviceIdType.MESH
F32 = jnp.float32
BF16 = jnp.bfloat16


def lane_ids(shape):
    return lax.broadcasted_iota(jnp.int32, shape, len(shape) - 1)


def rms(values, gain):
    wide = values.astype(F32)
    factor = lax.rsqrt(jnp.mean(wide * wide, axis=-1, keepdims=True) + 1e-05)
    return (wide * factor * gain).astype(BF16)


def dot(a, b):
    return jnp.dot(a, b, preferred_element_type=F32)


def dot_t(a, b):
    return lax.dot_general(a, b, (((1,), (1,)), ((), ())), preferred_element_type=F32)


def rotate(x, cosine, sine):
    width = x.shape[-1]
    low = lane_ids(x.shape) % HD < HD // 2
    ahead = pltpu.roll(x, width - HD // 2, 1)
    behind = pltpu.roll(x, HD // 2, 1)
    return x * cosine + jnp.where(low, -ahead, behind) * sine


def spread(q, local_kv):
    rows = q.shape[0]
    half = lane_ids((rows, 128)) < HD
    quarter = lane_ids((rows, WIDE)) // HD
    blocks = []
    for s, kv in enumerate(local_kv):
        pair = q[:, 128 * (s // 2) : 128 * (s // 2) + 128]
        turned = pltpu.roll(pair, HD, 1)
        both = jnp.where(half, pair, turned) if s % 2 == 0 else jnp.where(half, turned, pair)
        wide = jnp.concatenate([both, both], axis=1)
        blocks.append(jnp.where(quarter == kv, wide, 0.0))
    return jnp.concatenate(blocks, axis=0)


def pack(mixed, tops, totals, local_kv, rows):
    lanes = lane_ids((rows, 128))
    quarter = lane_ids((rows, WIDE)) // HD
    both = []
    for s, kv in enumerate(local_kv):
        part = jnp.where(quarter == kv, mixed[s * rows : (s + 1) * rows], 0.0)
        part = part[:, :128] + part[:, 128:]
        both.append(part + pltpu.roll(part, HD, 1))
    last = both[4]
    for s in range(5):
        top = tops[s * rows : (s + 1) * rows]
        total = totals[s * rows : (s + 1) * rows]
        last = jnp.where(lanes == HD + s, top, last)
        last = jnp.where(lanes == HD + 8 + s, total, last)
    return jnp.concatenate(
        [
            jnp.where(lanes < HD, both[0], both[1]),
            jnp.where(lanes < HD, both[2], both[3]),
            jnp.where((lanes < HD) | (lanes < HD + 16), last, 0.0),
        ],
        axis=1,
    )


def column(ref, start, rows):
    ids = lax.broadcasted_iota(jnp.int32, (8, 1), 0)
    blocks = []
    for block in range(rows // 8):
        col = jnp.zeros((8, 1), jnp.int32)
        for r in range(8):
            col = jnp.where(ids == r, ref[start + block * 8 + r], col)
        blocks.append(col)
    return blocks[0] if len(blocks) == 1 else jnp.concatenate(blocks, axis=0)


def kernel(
    n_seq,
    n_tp,
    tokens_h,
    attn_gain_h,
    w_query_h,
    w_key_h,
    w_value_h,
    w_out_h,
    prefix_keys_h,
    prefix_values_h,
    suffix_keys_h,
    suffix_values_h,
    group_of,
    prefix_len,
    suffix_len,
    mlp_gain_h,
    w_gate_h,
    w_up_h,
    w_down_h,
    out_ref,
    tokens,
    attn_gain,
    w_query,
    w_key,
    w_value,
    w_out,
    keys,
    values,
    suf_keys,
    suf_values,
    mlp_gain,
    w_gate,
    w_up,
    w_down,
    queries,
    send_parts,
    parts,
    head_parts,
    down_parts,
    local_sem,
    group_sem,
    q_send,
    q_recv,
    p_send,
    p_recv,
    h_send,
    h_recv,
    d_send,
    d_recv,
):
    seq = lax.axis_index("seq")
    tp = lax.axis_index("tp")
    rows = tokens.shape[0]
    groups, span = keys.shape[0], keys.shape[1]
    suffix_span = suf_keys.shape[1]

    barrier = pltpu.get_barrier_semaphore()

    def greet(k, carry):
        pl.semaphore_signal(
            barrier, inc=1, device_id={"seq": lax.rem(seq + k, n_seq)}, device_id_type=MESH
        )
        return carry

    if n_seq <= 8:
        for k in range(1, n_seq):
            greet(k, 0)
    else:
        lax.fori_loop(1, n_seq, greet, 0)
    for k in range(1, n_tp):
        pl.semaphore_signal(
            barrier, inc=1, device_id={"tp": lax.rem(tp + k, n_tp)}, device_id_type=MESH
        )

    per, surplus = HEADS // n_tp, HEADS % n_tp
    first_head = per * tp + jnp.minimum(tp, surplus)
    used = per + (tp < surplus).astype(jnp.int32)
    share = HEADS // KV_HEADS
    first_block = jnp.minimum((first_head // share) // 2, 1)
    local_kv = [
        jnp.minimum(first_head + s, HEADS - 1) // share - 2 * first_block for s in range(5)
    ]
    columns = pl.ds(pl.multiple_of(first_block * 128, 128), WIDE)

    copies = {}
    for i, (name, src, dst) in enumerate(
        [
            ("tokens", tokens_h, tokens),
            ("attn_gain", attn_gain_h, attn_gain),
            ("w_query", w_query_h, w_query),
            ("w_key", w_key_h.at[:, columns], w_key),
            ("w_value", w_value_h.at[:, columns], w_value),
            ("suf_keys", suffix_keys_h.at[:, :, columns], suf_keys),
            ("suf_values", suffix_values_h.at[:, :, columns], suf_values),
            ("w_out", w_out_h, w_out),
            ("mlp_gain", mlp_gain_h, mlp_gain),
            ("w_gate", w_gate_h, w_gate),
            ("w_up", w_up_h, w_up),
            ("w_down", w_down_h, w_down),
        ]
    ):
        copies[name] = pltpu.make_async_copy(src, dst, local_sem.at[i])
    key_copies = [
        pltpu.make_async_copy(prefix_keys_h.at[g, :, columns], keys.at[g], group_sem.at[0, g])
        for g in range(groups)
    ]
    value_copies = [
        pltpu.make_async_copy(prefix_values_h.at[g, :, columns], values.at[g], group_sem.at[1, g])
        for g in range(groups)
    ]
    for name in ("tokens", "attn_gain", "w_query", "w_key", "w_value", "suf_keys", "suf_values"):
        copies[name].start()
    for g in range(groups):
        key_copies[g].start()
        value_copies[g].start()
    for name in ("w_out", "mlp_gain", "w_gate", "w_up", "w_down"):
        copies[name].start()

    own_start = seq * rows
    own_group = column(group_of, own_start, rows)
    own_suffix = column(suffix_len, own_start, rows)
    own_prefix = jnp.zeros((rows, 1), jnp.int32)
    for g in range(groups):
        own_prefix = jnp.where(own_group == g, prefix_len[g], own_prefix)
    position = (own_prefix + own_suffix).astype(F32)
    turn = lane_ids((rows, 128)) % (HD // 2)
    frequency = jnp.ones((rows, 128), F32)
    for bit in range(5):
        step = 10000.0 ** (-(2**bit) / 32.0)
        frequency = jnp.where((turn // 2**bit) % 2 == 1, frequency * step, frequency)
    angles = position * frequency
    cosine, sine = jnp.cos(angles), jnp.sin(angles)
    cos2 = jnp.concatenate([cosine, cosine], axis=1)
    sin2 = jnp.concatenate([sine, sine], axis=1)
    cos3 = jnp.concatenate([cos2, cosine], axis=1)
    sin3 = jnp.concatenate([sin2, sine], axis=1)

    copies["tokens"].wait()
    copies["attn_gain"].wait()
    normed = rms(tokens[...], attn_gain[...])
    copies["w_query"].wait()
    q = dot(normed, w_query[...])
    q = jnp.concatenate([q, jnp.zeros((rows, PACK - q.shape[1]), F32)], axis=1)
    q_own = rotate(q, cos3, sin3).astype(BF16)
    queries[seq] = q_own
    pl.semaphore_wait(barrier, n_seq - 1 + n_tp - 1)

    def seq_copy(src, dst, send, recv, k):
        return pltpu.make_async_remote_copy(
            src_ref=src,
            dst_ref=dst,
            send_sem=send.at[k],
            recv_sem=recv.at[seq],
            device_id={"seq": lax.rem(seq + k, n_seq)},
            device_id_type=MESH,
        )

    def seq_wait(buf, send, recv, k):
        other = lax.rem(seq + k, n_seq)
        return pltpu.make_async_remote_copy(
            src_ref=buf.at[other],
            dst_ref=buf.at[other],
            send_sem=send.at[k],
            recv_sem=recv.at[other],
            device_id={"seq": other},
            device_id_type=MESH,
        )

    def over_peers(act):
        if n_seq <= 8:
            for k in range(1, n_seq):
                act(k)
        else:

            def step(k, carry):
                act(k)
                return carry

            lax.fori_loop(1, n_seq, step, 0)

    over_peers(
        lambda k: seq_copy(queries.at[seq], queries.at[seq], q_send, q_recv, k).start()
    )

    copies["w_key"].wait()
    copies["w_value"].wait()
    new_keys = rotate(dot(normed, w_key[...]), cos2, sin2).astype(BF16).astype(F32)
    new_values = dot(normed, w_value[...]).astype(BF16).astype(F32)
    q_wide = spread(q_own.astype(F32) * HD ** (-0.5), local_kv)
    own_score = jnp.sum(q_wide * jnp.concatenate([new_keys] * 5, axis=0), axis=1, keepdims=True)
    copies["suf_keys"].wait()
    suf_all = suf_keys[...].reshape(rows * suffix_span, WIDE)
    suf_scores = dot_t(q_wide.astype(BF16), suf_all)
    shape = suf_scores.shape
    spot = lane_ids(shape)
    row_id = lax.broadcasted_iota(jnp.int32, shape, 0) % rows
    limit = jnp.concatenate([own_suffix] * 5, axis=0)
    suf_live = (spot >= row_id * suffix_span) & (spot < row_id * suffix_span + limit)
    suf_scores = jnp.where(suf_live, suf_scores, NEG)
    suf_top = jnp.maximum(jnp.max(suf_scores, axis=1, keepdims=True), own_score)
    suf_weights = jnp.exp(suf_scores - suf_top)
    own_weight = jnp.exp(own_score - suf_top)
    suf_total = jnp.sum(suf_weights, axis=1, keepdims=True) + own_weight
    copies["suf_values"].wait()
    suf_mixed = dot(suf_weights.astype(BF16), suf_values[...].reshape(rows * suffix_span, WIDE))
    own_low = own_weight.astype(BF16).astype(F32)
    suf_mixed = suf_mixed + own_low * jnp.concatenate([new_values] * 5, axis=0)
    suf_part = pack(suf_mixed, suf_top, suf_total, local_kv, rows)

    over_peers(lambda k: seq_wait(queries, q_send, q_recv, k).wait_recv())
    for g in range(groups):
        key_copies[g].wait()
        value_copies[g].wait()

    per_chunk = min(8, n_seq)
    chunk_rows = per_chunk * rows
    spots = seq * span + lane_ids((1, span))

    def prefix_chunk(c, carry):
        q_all = queries[pl.ds(c * per_chunk, per_chunk)].astype(F32).reshape(chunk_rows, PACK)
        q_all = spread(q_all * HD ** (-0.5), local_kv).astype(BF16)
        group = column(group_of, c * chunk_rows, chunk_rows)
        group = jnp.concatenate([group] * 5, axis=0)
        mixed = jnp.zeros((5 * chunk_rows, WIDE), F32)
        tops = jnp.full((5 * chunk_rows, 1), NEG, F32)
        totals = jnp.zeros((5 * chunk_rows, 1), F32)
        for g in range(groups):
            scores = jnp.where(spots < prefix_len[g], dot_t(q_all, keys[g]), NEG)
            top = jnp.max(scores, axis=1, keepdims=True)
            member = group == g
            tops = jnp.where(member, top, tops)
            weights = jnp.exp(scores - jnp.where(member, top, -NEG))
            totals += jnp.sum(weights, axis=1, keepdims=True)
            mixed += dot(weights.astype(BF16), values[g])
        packed = pack(mixed, tops, totals, local_kv, chunk_rows)
        send_parts[pl.ds(c * per_chunk, per_chunk)] = packed.reshape(per_chunk, rows, PACK)
        return carry

    if n_seq == per_chunk:
        prefix_chunk(0, 0)
    else:
        lax.fori_loop(0, n_seq // per_chunk, prefix_chunk, 0)

    def send_part(k):
        other = lax.rem(seq + k, n_seq)
        seq_copy(send_parts.at[other], parts.at[seq], p_send, p_recv, k).start()

    over_peers(send_part)
    parts[seq] = send_parts[seq]
    over_peers(lambda k: seq_wait(parts, p_send, p_recv, k).wait_recv())

    every = parts[...]
    ends = every[:, :, 256:]
    suf_end = suf_part[:, 256:]
    top = jnp.maximum(jnp.max(ends, axis=0), suf_end)
    scales = jnp.exp(ends - top[None])
    suf_scale = jnp.exp(suf_end - top)
    total = suf_scale * pltpu.roll(suf_end, 120, 1)
    for i in range(n_seq):
        total = total + scales[i] * pltpu.roll(ends[i], 120, 1)
    used_lane = lane_ids((rows, 128)) - HD < used
    share_of = jnp.where(used_lane, 1.0 / total, 0.0)
    half = lane_ids((rows, 128)) < HD

    def weigh(scale, part):
        scale = scale * share_of
        cols = [scale[:, HD + s : HD + s + 1] for s in range(5)]
        return jnp.concatenate(
            [
                jnp.where(half, cols[0], cols[1]) * part[:, :128],
                jnp.where(half, cols[2], cols[3]) * part[:, 128:256],
                jnp.where(half, cols[4], 0.0) * part[:, 256:],
            ],
            axis=1,
        )

    attended = weigh(suf_scale, suf_part)
    for i in range(n_seq):
        attended = attended + weigh(scales[i], every[i])
    attended = attended[:, : 5 * HD].astype(BF16)

    def tp_sum(buf, send, recv):
        for k in range(1, n_tp):
            pltpu.make_async_remote_copy(
                src_ref=buf.at[tp],
                dst_ref=buf.at[tp],
                send_sem=send.at[k],
                recv_sem=recv.at[tp],
                device_id={"tp": lax.rem(tp + k, n_tp)},
                device_id_type=MESH,
            ).start()
        for k in range(1, n_tp):
            other = lax.rem(tp + k, n_tp)
            pltpu.make_async_remote_copy(
                src_ref=buf.at[other],
                dst_ref=buf.at[other],
                send_sem=send.at[k],
                recv_sem=recv.at[other],
                device_id={"tp": other},
                device_id_type=MESH,
            ).wait_recv()
        total = buf[0].astype(F32)
        for i in range(1, n_tp):
            total = total + buf[i].astype(F32)
        return total

    copies["w_out"].wait()
    head_parts[tp] = dot(attended, w_out[...]).astype(BF16)
    hidden = (tokens[...].astype(F32) + tp_sum(head_parts, h_send, h_recv)).astype(BF16)
    copies["mlp_gain"].wait()
    mlp_in = rms(hidden, mlp_gain[...])
    copies["w_gate"].wait()
    gate = dot(mlp_in, w_gate[...])
    copies["w_up"].wait()
    up = dot(mlp_in, w_up[...])
    activation = (gate / (1.0 + jnp.exp(-gate)) * up).astype(BF16)
    copies["w_down"].wait()
    down_parts[tp] = dot(activation, w_down[...]).astype(BF16)
    total = tp_sum(down_parts, d_send, d_recv)
    out_ref[...] = (hidden.astype(F32) + total).astype(BF16)

    over_peers(
        lambda k: seq_copy(queries.at[seq], queries.at[seq], q_send, q_recv, k).wait_send()
    )

    def sent_part(k):
        other = lax.rem(seq + k, n_seq)
        seq_copy(send_parts.at[other], parts.at[seq], p_send, p_recv, k).wait_send()

    over_peers(sent_part)
    for buf, send, recv in ((head_parts, h_send, h_recv), (down_parts, d_send, d_recv)):
        for k in range(1, n_tp):
            pltpu.make_async_remote_copy(
                src_ref=buf.at[tp],
                dst_ref=buf.at[tp],
                send_sem=send.at[k],
                recv_sem=recv.at[tp],
                device_id={"tp": lax.rem(tp + k, n_tp)},
                device_id_type=MESH,
            ).wait_send()


def on_device(n_seq, n_tp, *args):
    tokens, w_query, w_out, w_gate, w_down = args[0], args[2], args[5], args[14], args[16]
    prefix, suffix = args[6], args[8]
    rows, width = tokens.shape
    groups, span, _ = prefix.shape
    hidden_units = w_gate.shape[1]
    dma = pltpu.SemaphoreType.DMA
    args = list(args)
    args[1] = args[1].reshape(1, width)
    args[13] = args[13].reshape(1, width)
    in_specs = [pl.BlockSpec(memory_space=pl.ANY)] * len(args)
    for i in (10, 11, 12):
        in_specs[i] = pl.BlockSpec(memory_space=pltpu.SMEM)
    return pl.pallas_call(
        functools.partial(kernel, n_seq, n_tp),
        out_shape=jax.ShapeDtypeStruct((rows, width), BF16),
        in_specs=in_specs,
        out_specs=pl.BlockSpec(memory_space=pltpu.VMEM),
        scratch_shapes=[
            pltpu.VMEM((rows, width), BF16),
            pltpu.VMEM((1, width), F32),
            pltpu.VMEM(w_query.shape, BF16),
            pltpu.VMEM((width, WIDE), BF16),
            pltpu.VMEM((width, WIDE), BF16),
            pltpu.VMEM(w_out.shape, BF16),
            pltpu.VMEM((groups, span, WIDE), BF16),
            pltpu.VMEM((groups, span, WIDE), BF16),
            pltpu.VMEM((rows, suffix.shape[1], WIDE), BF16),
            pltpu.VMEM((rows, suffix.shape[1], WIDE), BF16),
            pltpu.VMEM((1, width), F32),
            pltpu.VMEM(w_gate.shape, BF16),
            pltpu.VMEM(w_gate.shape, BF16),
            pltpu.VMEM(w_down.shape, BF16),
            pltpu.VMEM((n_seq, rows, PACK), BF16),
            pltpu.VMEM((n_seq, rows, PACK), F32),
            pltpu.VMEM((n_seq, rows, PACK), F32),
            pltpu.VMEM((n_tp, rows, width), BF16),
            pltpu.VMEM((n_tp, rows, width), BF16),
            dma((12,)),
            dma((2, groups)),
            dma((n_seq,)),
            dma((n_seq,)),
            dma((n_seq,)),
            dma((n_seq,)),
            dma((n_tp,)),
            dma((n_tp,)),
            dma((n_tp,)),
            dma((n_tp,)),
        ],
        compiler_params=pltpu.CompilerParams(
            collective_id=0, has_side_effects=True, vmem_limit_bytes=56 * 1024 * 1024
        ),
    )(*args)


def solution(mesh):
    return jax.shard_map(
        functools.partial(on_device, mesh.shape["seq"], mesh.shape["tp"]),
        mesh=mesh,
        in_specs=(
            P("seq", None),
            P(),
            P(None, "tp"),
            P(),
            P(),
            P("tp", None),
            P(None, "seq", None),
            P(None, "seq", None),
            P("seq", None, None),
            P("seq", None, None),
            P(),
            P(),
            P(),
            P(),
            P(None, "tp"),
            P(None, "tp"),
            P("tp", None),
        ),
        out_specs=P("seq", None),
        check_vma=False,
    )
```

```python
import functools

import jax
import jax.numpy as jnp
from jax import lax
from jax.experimental import pallas as pl
from jax.experimental.pallas import tpu as pltpu
from jax.sharding import PartitionSpec as P

HEADS = 18
KV_HEADS = 6
HD = 64
NEG = -1e30
WIDE = 256
PACK = 384
MESH = pl.DeviceIdType.MESH
F32 = jnp.float32
BF16 = jnp.bfloat16


def lane_ids(shape):
    return lax.broadcasted_iota(jnp.int32, shape, len(shape) - 1)


def rms(values, gain):
    wide = values.astype(F32)
    factor = lax.rsqrt(jnp.mean(wide * wide, axis=-1, keepdims=True) + 1e-05)
    return (wide * factor * gain).astype(BF16)


def dot(a, b):
    return jnp.dot(a, b, preferred_element_type=F32)


def dot_t(a, b):
    return lax.dot_general(a, b, (((1,), (1,)), ((), ())), preferred_element_type=F32)


def rotate(x, cosine, sine):
    width = x.shape[-1]
    low = lane_ids(x.shape) % HD < HD // 2
    ahead = pltpu.roll(x, width - HD // 2, 1)
    behind = pltpu.roll(x, HD // 2, 1)
    return x * cosine + jnp.where(low, -ahead, behind) * sine


def spread(q, local_kv):
    rows = q.shape[0]
    half = lane_ids((rows, 128)) < HD
    quarter = lane_ids((rows, WIDE)) // HD
    blocks = []
    for s, kv in enumerate(local_kv):
        pair = q[:, 128 * (s // 2) : 128 * (s // 2) + 128]
        turned = pltpu.roll(pair, HD, 1)
        both = jnp.where(half, pair, turned) if s % 2 == 0 else jnp.where(half, turned, pair)
        wide = jnp.concatenate([both, both], axis=1)
        blocks.append(jnp.where(quarter == kv, wide, 0.0))
    return jnp.concatenate(blocks, axis=0)


def pack(mixed, tops, totals, local_kv, rows):
    lanes = lane_ids((rows, 128))
    quarter = lane_ids((rows, WIDE)) // HD
    both = []
    for s, kv in enumerate(local_kv):
        part = jnp.where(quarter == kv, mixed[s * rows : (s + 1) * rows], 0.0)
        part = part[:, :128] + part[:, 128:]
        both.append(part + pltpu.roll(part, HD, 1))
    top_row = jnp.zeros((rows, 128), F32)
    total_row = jnp.zeros((rows, 128), F32)
    for s in range(5):
        top_row = jnp.where(lanes == HD + s, tops[s * rows : (s + 1) * rows], top_row)
        total_row = jnp.where(lanes == HD + s, totals[s * rows : (s + 1) * rows], total_row)
    blocks = [
        jnp.where(lanes < HD, both[0], both[1]),
        jnp.where(lanes < HD, both[2], both[3]),
        jnp.where(lanes < HD, both[4], 0.0),
    ]
    return blocks, top_row, total_row


def terms(x):
    high = x.astype(BF16).astype(F32)
    middle = (x - high).astype(BF16).astype(F32)
    return high, middle, x - high - middle


def fold_lanes(x):
    out = x[:, :128]
    for i in range(128, x.shape[1], 128):
        out = out + x[:, i : i + 128]
    return out


def fold_max(x):
    out = x[:, :128]
    for i in range(128, x.shape[1], 128):
        out = jnp.maximum(out, x[:, i : i + 128])
    return out


def column(ref, start, rows):
    ids = lax.broadcasted_iota(jnp.int32, (8, 1), 0)
    blocks = []
    for block in range(rows // 8):
        col = jnp.zeros((8, 1), jnp.int32)
        for r in range(8):
            col = jnp.where(ids == r, ref[start + block * 8 + r], col)
        blocks.append(col)
    return blocks[0] if len(blocks) == 1 else jnp.concatenate(blocks, axis=0)


def kernel(
    n_seq,
    n_tp,
    tokens_h,
    attn_gain_h,
    w_query_h,
    w_key_h,
    w_value_h,
    w_out_h,
    prefix_keys_h,
    prefix_values_h,
    suffix_keys_h,
    suffix_values_h,
    group_of,
    prefix_len,
    suffix_len,
    mlp_gain_h,
    w_gate_h,
    w_up_h,
    w_down_h,
    out_ref,
    tokens,
    attn_gain,
    w_query,
    w_key,
    w_value,
    w_out,
    keys,
    values,
    suf_keys,
    suf_values,
    mlp_gain,
    w_gate,
    w_up,
    w_down,
    queries,
    send_parts,
    parts,
    all_scores,
    head_parts,
    down_parts,
    local_sem,
    group_sem,
    q_send,
    q_recv,
    p_send,
    p_recv,
    h_send,
    h_recv,
    d_send,
    d_recv,
):
    seq = lax.axis_index("seq")
    tp = lax.axis_index("tp")
    rows = tokens.shape[0]
    groups, span = keys.shape[0], keys.shape[1]
    suffix_span = suf_keys.shape[1]

    barrier = pltpu.get_barrier_semaphore()

    def greet(k, carry):
        pl.semaphore_signal(
            barrier, inc=1, device_id={"seq": lax.rem(seq + k, n_seq)}, device_id_type=MESH
        )
        return carry

    if n_seq <= 8:
        for k in range(1, n_seq):
            greet(k, 0)
    else:
        lax.fori_loop(1, n_seq, greet, 0)
    for k in range(1, n_tp):
        pl.semaphore_signal(
            barrier, inc=1, device_id={"tp": lax.rem(tp + k, n_tp)}, device_id_type=MESH
        )

    per, surplus = HEADS // n_tp, HEADS % n_tp
    first_head = per * tp + jnp.minimum(tp, surplus)
    used = per + (tp < surplus).astype(jnp.int32)
    share = HEADS // KV_HEADS
    first_block = jnp.minimum((first_head // share) // 2, 1)
    local_kv = [
        jnp.minimum(first_head + s, HEADS - 1) // share - 2 * first_block for s in range(5)
    ]
    columns = pl.ds(pl.multiple_of(first_block * 128, 128), WIDE)

    copies = {}
    for i, (name, src, dst) in enumerate(
        [
            ("tokens", tokens_h, tokens),
            ("attn_gain", attn_gain_h, attn_gain),
            ("w_query", w_query_h, w_query),
            ("w_key", w_key_h.at[:, columns], w_key),
            ("w_value", w_value_h.at[:, columns], w_value),
            ("suf_keys", suffix_keys_h.at[:, :, columns], suf_keys),
            ("suf_values", suffix_values_h.at[:, :, columns], suf_values),
            ("w_out", w_out_h, w_out),
            ("mlp_gain", mlp_gain_h, mlp_gain),
            ("w_gate", w_gate_h, w_gate),
            ("w_up", w_up_h, w_up),
            ("w_down", w_down_h, w_down),
        ]
    ):
        copies[name] = pltpu.make_async_copy(src, dst, local_sem.at[i])
    key_copies = [
        pltpu.make_async_copy(prefix_keys_h.at[g, :, columns], keys.at[g], group_sem.at[0, g])
        for g in range(groups)
    ]
    value_copies = [
        pltpu.make_async_copy(prefix_values_h.at[g, :, columns], values.at[g], group_sem.at[1, g])
        for g in range(groups)
    ]
    for name in ("tokens", "attn_gain", "w_query", "w_key", "w_value", "suf_keys", "suf_values"):
        copies[name].start()
    for g in range(groups):
        key_copies[g].start()
        value_copies[g].start()
    for name in ("w_out", "mlp_gain", "w_gate", "w_up", "w_down"):
        copies[name].start()

    own_start = seq * rows
    own_group = column(group_of, own_start, rows)
    own_suffix = column(suffix_len, own_start, rows)
    own_prefix = jnp.zeros((rows, 1), jnp.int32)
    for g in range(groups):
        own_prefix = jnp.where(own_group == g, prefix_len[g], own_prefix)
    position = (own_prefix + own_suffix).astype(F32)
    turn = lane_ids((rows, 128)) % (HD // 2)
    frequency = jnp.ones((rows, 128), F32)
    for bit in range(5):
        step = 10000.0 ** (-(2**bit) / 32.0)
        frequency = jnp.where((turn // 2**bit) % 2 == 1, frequency * step, frequency)
    angles = position * frequency
    cosine, sine = jnp.cos(angles), jnp.sin(angles)
    cos2 = jnp.concatenate([cosine, cosine], axis=1)
    sin2 = jnp.concatenate([sine, sine], axis=1)
    cos3 = jnp.concatenate([cos2, cosine], axis=1)
    sin3 = jnp.concatenate([sin2, sine], axis=1)

    copies["tokens"].wait()
    copies["attn_gain"].wait()
    normed = rms(tokens[...], attn_gain[...].reshape(1, tokens.shape[1]))
    copies["w_query"].wait()
    q = dot_t(normed, w_query[...])
    q = jnp.concatenate([q, jnp.zeros((rows, PACK - q.shape[1]), F32)], axis=1)
    q_own = rotate(q, cos3, sin3).astype(BF16)
    queries[seq] = q_own
    pl.semaphore_wait(barrier, n_seq - 1 + n_tp - 1)

    def seq_copy(src, dst, send, recv, k):
        return pltpu.make_async_remote_copy(
            src_ref=src,
            dst_ref=dst,
            send_sem=send.at[k],
            recv_sem=recv.at[seq],
            device_id={"seq": lax.rem(seq + k, n_seq)},
            device_id_type=MESH,
        )

    def seq_wait(buf, send, recv, k):
        other = lax.rem(seq + k, n_seq)
        return pltpu.make_async_remote_copy(
            src_ref=buf.at[other],
            dst_ref=buf.at[other],
            send_sem=send.at[k],
            recv_sem=recv.at[other],
            device_id={"seq": other},
            device_id_type=MESH,
        )

    def over_peers(act):
        if n_seq <= 8:
            for k in range(1, n_seq):
                act(k)
        else:

            def step(k, carry):
                act(k)
                return carry

            lax.fori_loop(1, n_seq, step, 0)

    over_peers(
        lambda k: seq_copy(queries.at[seq], queries.at[seq], q_send, q_recv, k).start()
    )

    copies["w_key"].wait()
    copies["w_value"].wait()
    new_keys = rotate(dot(normed, w_key[...]), cos2, sin2).astype(BF16).astype(F32)
    new_values = dot(normed, w_value[...]).astype(BF16).astype(F32)
    q_wide = spread(q_own.astype(F32) * HD ** (-0.5), local_kv)
    own_score = jnp.sum(q_wide * jnp.concatenate([new_keys] * 5, axis=0), axis=1, keepdims=True)
    copies["suf_keys"].wait()
    suf_all = suf_keys[...].reshape(rows * suffix_span, WIDE)
    suf_scores = dot_t(q_wide.astype(BF16), suf_all)
    shape = suf_scores.shape
    spot = lane_ids(shape)
    row_id = lax.broadcasted_iota(jnp.int32, shape, 0) % rows
    limit = jnp.concatenate([own_suffix] * 5, axis=0)
    suf_live = (spot >= row_id * suffix_span) & (spot < row_id * suffix_span + limit)
    suf_scores = jnp.where(suf_live, suf_scores, NEG)
    suf_top = jnp.maximum(jnp.max(suf_scores, axis=1, keepdims=True), own_score)
    suf_weights = jnp.exp(suf_scores - suf_top)
    own_weight = jnp.exp(own_score - suf_top)
    suf_total = jnp.sum(suf_weights, axis=1, keepdims=True) + own_weight
    copies["suf_values"].wait()
    suf_mixed = dot(suf_weights.astype(BF16), suf_values[...].reshape(rows * suffix_span, WIDE))
    own_low = own_weight.astype(BF16).astype(F32)
    suf_mixed = suf_mixed + own_low * jnp.concatenate([new_values] * 5, axis=0)
    suf_blocks, suf_end, suf_sum = pack(suf_mixed, suf_top, suf_total, local_kv, rows)

    over_peers(lambda k: seq_wait(queries, q_send, q_recv, k).wait_recv())
    for g in range(groups):
        key_copies[g].wait()
        value_copies[g].wait()

    per_chunk = min(8, n_seq)
    chunk_rows = per_chunk * rows
    spots = seq * span + lane_ids((1, span))

    def prefix_chunk(c, carry):
        q_all = queries[pl.ds(c * per_chunk, per_chunk)].astype(F32).reshape(chunk_rows, PACK)
        q_all = spread(q_all * HD ** (-0.5), local_kv).astype(BF16)
        group = column(group_of, c * chunk_rows, chunk_rows)
        group = jnp.concatenate([group] * 5, axis=0)
        mixed = jnp.zeros((5 * chunk_rows, WIDE), F32)
        peaks = jnp.full((5 * chunk_rows, 128), NEG, F32)
        for g in range(groups):
            scores = jnp.where(spots < prefix_len[g], dot_t(q_all, keys[g]), NEG)
            all_scores[g] = scores
            peaks = jnp.where(group == g, fold_max(scores), peaks)
        tops = jnp.max(peaks, axis=1, keepdims=True)
        sums = jnp.zeros((5 * chunk_rows, 128), F32)
        for g in range(groups):
            weights = jnp.exp(all_scores[g] - jnp.where(group == g, tops, -NEG))
            sums += fold_lanes(weights)
            mixed += dot(weights.astype(BF16), values[g])
        totals = jnp.sum(sums, axis=1, keepdims=True)
        blocks, top_row, total_row = pack(mixed, tops, totals, local_kv, chunk_rows)
        for i, term in enumerate(terms(top_row) + terms(total_row)):
            blocks[2] = blocks[2] + (term if i == 0 else pltpu.roll(term, 8 * i, 1))
        packed = jnp.concatenate(blocks, axis=1).reshape(per_chunk, rows, PACK)
        send_parts[pl.ds(c * per_chunk, per_chunk)] = packed.astype(BF16)
        return carry

    if n_seq == per_chunk:
        prefix_chunk(0, 0)
    else:
        lax.fori_loop(0, n_seq // per_chunk, prefix_chunk, 0)

    def send_part(k):
        other = lax.rem(seq + k, n_seq)
        seq_copy(send_parts.at[other], parts.at[seq], p_send, p_recv, k).start()

    over_peers(send_part)
    parts[seq] = send_parts[seq]
    over_peers(lambda k: seq_wait(parts, p_send, p_recv, k).wait_recv())

    every = parts[...].astype(F32)
    ends = every[:, :, 256:].reshape(n_seq * rows, 128)
    rolled = [ends] + [pltpu.roll(ends, 128 - 8 * i, 1) for i in range(1, 6)]
    part_tops = (rolled[0] + rolled[1] + rolled[2]).reshape(n_seq, rows, 128)
    part_sums = (rolled[3] + rolled[4] + rolled[5]).reshape(n_seq, rows, 128)
    top = jnp.maximum(jnp.max(part_tops, axis=0), suf_end)
    scales = jnp.exp(part_tops - top[None])
    suf_scale = jnp.exp(suf_end - top)
    total = suf_scale * suf_sum + jnp.sum(scales * part_sums, axis=0)
    used_lane = lane_ids((rows, 128)) - HD < used
    share_of = jnp.where(used_lane, 1.0 / total, 0.0)
    half = lane_ids((rows, 128)) < HD

    def weigh(scale, part):
        scale = scale * share_of
        cols = [scale[:, HD + s : HD + s + 1] for s in range(5)]
        return jnp.concatenate(
            [
                jnp.where(half, cols[0], cols[1]) * part[:, :128],
                jnp.where(half, cols[2], cols[3]) * part[:, 128:256],
                jnp.where(half, cols[4], 0.0) * part[:, 256:],
            ],
            axis=1,
        )

    attended = weigh(suf_scale, jnp.concatenate(suf_blocks, axis=1))
    for i in range(n_seq):
        attended = attended + weigh(scales[i], every[i])
    attended = attended[:, : 5 * HD].astype(BF16)

    def tp_sum(buf, send, recv):
        for k in range(1, n_tp):
            pltpu.make_async_remote_copy(
                src_ref=buf.at[tp],
                dst_ref=buf.at[tp],
                send_sem=send.at[k],
                recv_sem=recv.at[tp],
                device_id={"tp": lax.rem(tp + k, n_tp)},
                device_id_type=MESH,
            ).start()
        for k in range(1, n_tp):
            other = lax.rem(tp + k, n_tp)
            pltpu.make_async_remote_copy(
                src_ref=buf.at[other],
                dst_ref=buf.at[other],
                send_sem=send.at[k],
                recv_sem=recv.at[other],
                device_id={"tp": other},
                device_id_type=MESH,
            ).wait_recv()
        total = buf[0].astype(F32)
        for i in range(1, n_tp):
            total = total + buf[i].astype(F32)
        return total

    copies["w_out"].wait()
    head_parts[tp] = dot(attended, w_out[...]).astype(BF16)
    hidden = (tokens[...].astype(F32) + tp_sum(head_parts, h_send, h_recv)).astype(BF16)
    copies["mlp_gain"].wait()
    mlp_in = rms(hidden, mlp_gain[...].reshape(1, tokens.shape[1]))
    copies["w_gate"].wait()
    gate = dot(mlp_in, w_gate[...])
    copies["w_up"].wait()
    up = dot(mlp_in, w_up[...])
    activation = (gate / (1.0 + jnp.exp(-gate)) * up).astype(BF16)
    copies["w_down"].wait()
    down_parts[tp] = dot(activation, w_down[...]).astype(BF16)
    total = tp_sum(down_parts, d_send, d_recv)
    out_ref[...] = (hidden.astype(F32) + total).astype(BF16)

    over_peers(
        lambda k: seq_copy(queries.at[seq], queries.at[seq], q_send, q_recv, k).wait_send()
    )

    def sent_part(k):
        other = lax.rem(seq + k, n_seq)
        seq_copy(send_parts.at[other], parts.at[seq], p_send, p_recv, k).wait_send()

    over_peers(sent_part)
    for buf, send, recv in ((head_parts, h_send, h_recv), (down_parts, d_send, d_recv)):
        for k in range(1, n_tp):
            pltpu.make_async_remote_copy(
                src_ref=buf.at[tp],
                dst_ref=buf.at[tp],
                send_sem=send.at[k],
                recv_sem=recv.at[tp],
                device_id={"tp": lax.rem(tp + k, n_tp)},
                device_id_type=MESH,
            ).wait_send()


def on_device(n_seq, n_tp, *args):
    tokens, w_query, w_out, w_gate, w_down = args[0], args[2], args[5], args[14], args[16]
    prefix, suffix = args[6], args[8]
    rows, width = tokens.shape
    groups, span, _ = prefix.shape
    hidden_units = w_gate.shape[1]
    dma = pltpu.SemaphoreType.DMA
    args = list(args)
    args[2] = w_query.T
    in_specs = [pl.BlockSpec(memory_space=pl.ANY)] * len(args)
    for i in (10, 11, 12):
        in_specs[i] = pl.BlockSpec(memory_space=pltpu.SMEM)
    return pl.pallas_call(
        functools.partial(kernel, n_seq, n_tp),
        out_shape=jax.ShapeDtypeStruct((rows, width), BF16),
        in_specs=in_specs,
        out_specs=pl.BlockSpec(memory_space=pltpu.VMEM),
        scratch_shapes=[
            pltpu.VMEM((rows, width), BF16),
            pltpu.VMEM((width,), F32),
            pltpu.VMEM(w_query.shape[::-1], BF16),
            pltpu.VMEM((width, WIDE), BF16),
            pltpu.VMEM((width, WIDE), BF16),
            pltpu.VMEM(w_out.shape, BF16),
            pltpu.VMEM((groups, span, WIDE), BF16),
            pltpu.VMEM((groups, span, WIDE), BF16),
            pltpu.VMEM((rows, suffix.shape[1], WIDE), BF16),
            pltpu.VMEM((rows, suffix.shape[1], WIDE), BF16),
            pltpu.VMEM((width,), F32),
            pltpu.VMEM(w_gate.shape, BF16),
            pltpu.VMEM(w_gate.shape, BF16),
            pltpu.VMEM(w_down.shape, BF16),
            pltpu.VMEM((n_seq, rows, PACK), BF16),
            pltpu.VMEM((n_seq, rows, PACK), BF16),
            pltpu.VMEM((n_seq, rows, PACK), BF16),
            pltpu.VMEM((groups, 5 * rows * min(8, n_seq), span), F32),
            pltpu.VMEM((n_tp, rows, width), BF16),
            pltpu.VMEM((n_tp, rows, width), BF16),
            dma((12,)),
            dma((2, groups)),
            dma((n_seq,)),
            dma((n_seq,)),
            dma((n_seq,)),
            dma((n_seq,)),
            dma((n_tp,)),
            dma((n_tp,)),
            dma((n_tp,)),
            dma((n_tp,)),
        ],
        compiler_params=pltpu.CompilerParams(
            collective_id=0, has_side_effects=True, vmem_limit_bytes=56 * 1024 * 1024
        ),
    )(*args)


def solution(mesh):
    return jax.shard_map(
        functools.partial(on_device, mesh.shape["seq"], mesh.shape["tp"]),
        mesh=mesh,
        in_specs=(
            P("seq", None),
            P(),
            P(None, "tp"),
            P(),
            P(),
            P("tp", None),
            P(None, "seq", None),
            P(None, "seq", None),
            P("seq", None, None),
            P("seq", None, None),
            P(),
            P(),
            P(),
            P(),
            P(None, "tp"),
            P(None, "tp"),
            P("tp", None),
        ),
        out_specs=P("seq", None),
        check_vma=False,
    )
```

```python
import functools

import jax
import jax.numpy as jnp
from jax import lax
from jax.experimental import pallas as pl
from jax.experimental.pallas import tpu as pltpu
from jax.sharding import PartitionSpec as P

HEADS = 18
KV_HEADS = 6
HD = 64
NEG = -1e30
WIDE = 256
PACK = 384
MESH = pl.DeviceIdType.MESH
F32 = jnp.float32
BF16 = jnp.bfloat16


def lane_ids(shape):
    return lax.broadcasted_iota(jnp.int32, shape, len(shape) - 1)


def rms(values, gain):
    wide = values.astype(F32)
    factor = lax.rsqrt(jnp.mean(wide * wide, axis=-1, keepdims=True) + 1e-05)
    return (wide * factor * gain).astype(BF16)


def dot(a, b):
    return jnp.dot(a, b, preferred_element_type=F32)


def dot_t(a, b):
    return lax.dot_general(a, b, (((1,), (1,)), ((), ())), preferred_element_type=F32)


def rotate(x, cosine, sine):
    width = x.shape[-1]
    low = lane_ids(x.shape) % HD < HD // 2
    ahead = pltpu.roll(x, width - HD // 2, 1)
    behind = pltpu.roll(x, HD // 2, 1)
    return x * cosine + jnp.where(low, -ahead, behind) * sine


def spread(q, local_kv):
    rows = q.shape[0]
    half = lane_ids((rows, 128)) < HD
    quarter = lane_ids((rows, WIDE)) // HD
    blocks = []
    for s, kv in enumerate(local_kv):
        pair = q[:, 128 * (s // 2) : 128 * (s // 2) + 128]
        turned = pltpu.roll(pair, HD, 1)
        both = jnp.where(half, pair, turned) if s % 2 == 0 else jnp.where(half, turned, pair)
        wide = jnp.concatenate([both, both], axis=1)
        blocks.append(jnp.where(quarter == kv, wide, 0.0))
    return jnp.concatenate(blocks, axis=0)


def pack(mixed, tops, totals, local_kv, rows):
    lanes = lane_ids((rows, 128))
    quarter = lane_ids((rows, WIDE)) // HD
    both = []
    for s, kv in enumerate(local_kv):
        part = jnp.where(quarter == kv, mixed[s * rows : (s + 1) * rows], 0.0)
        part = part[:, :128] + part[:, 128:]
        both.append(part + pltpu.roll(part, HD, 1))
    top_row = jnp.zeros((rows, 128), F32)
    total_row = jnp.zeros((rows, 128), F32)
    for s in range(5):
        top_row = jnp.where(lanes == HD + s, tops[s * rows : (s + 1) * rows], top_row)
        total_row = jnp.where(lanes == HD + s, totals[s * rows : (s + 1) * rows], total_row)
    blocks = [
        jnp.where(lanes < HD, both[0], both[1]),
        jnp.where(lanes < HD, both[2], both[3]),
        jnp.where(lanes < HD, both[4], 0.0),
    ]
    return blocks, top_row, total_row


def terms(x):
    high = x.astype(BF16).astype(F32)
    middle = (x - high).astype(BF16).astype(F32)
    return high, middle, x - high - middle


def fold_lanes(x):
    out = x[:, :128]
    for i in range(128, x.shape[1], 128):
        out = out + x[:, i : i + 128]
    return out


def fold_max(x):
    out = x[:, :128]
    for i in range(128, x.shape[1], 128):
        out = jnp.maximum(out, x[:, i : i + 128])
    return out


def column(ref, start, rows):
    ids = lax.broadcasted_iota(jnp.int32, (8, 1), 0)
    blocks = []
    for block in range(rows // 8):
        col = jnp.zeros((8, 1), jnp.int32)
        for r in range(8):
            col = jnp.where(ids == r, ref[start + block * 8 + r], col)
        blocks.append(col)
    return blocks[0] if len(blocks) == 1 else jnp.concatenate(blocks, axis=0)


def kernel(
    n_seq,
    n_tp,
    tokens_h,
    attn_gain_h,
    w_query_h,
    w_key_h,
    w_value_h,
    w_out_h,
    prefix_keys_h,
    prefix_values_h,
    suffix_keys_h,
    suffix_values_h,
    group_of,
    prefix_len,
    suffix_len,
    mlp_gain_h,
    w_gate_h,
    w_up_h,
    w_down_h,
    out_ref,
    tokens,
    attn_gain,
    w_query,
    w_key,
    w_value,
    w_out,
    keys,
    values,
    suf_keys,
    suf_values,
    mlp_gain,
    w_gate,
    w_up,
    w_down,
    queries,
    send_parts,
    parts,
    head_parts,
    down_parts,
    local_sem,
    group_sem,
    q_send,
    q_recv,
    p_send,
    p_recv,
    h_send,
    h_recv,
    d_send,
    d_recv,
):
    seq = lax.axis_index("seq")
    tp = lax.axis_index("tp")
    rows = tokens.shape[0]
    groups, span = keys.shape[0], keys.shape[1]
    suffix_span = suf_keys.shape[1]

    barrier = pltpu.get_barrier_semaphore()

    def greet(k, carry):
        pl.semaphore_signal(
            barrier, inc=1, device_id={"seq": lax.rem(seq + k, n_seq)}, device_id_type=MESH
        )
        return carry

    if n_seq <= 8:
        for k in range(1, n_seq):
            greet(k, 0)
    else:
        lax.fori_loop(1, n_seq, greet, 0)
    for k in range(1, n_tp):
        pl.semaphore_signal(
            barrier, inc=1, device_id={"tp": lax.rem(tp + k, n_tp)}, device_id_type=MESH
        )

    per, surplus = HEADS // n_tp, HEADS % n_tp
    first_head = per * tp + jnp.minimum(tp, surplus)
    used = per + (tp < surplus).astype(jnp.int32)
    share = HEADS // KV_HEADS
    first_block = jnp.minimum((first_head // share) // 2, 1)
    local_kv = [
        jnp.minimum(first_head + s, HEADS - 1) // share - 2 * first_block for s in range(5)
    ]
    columns = pl.ds(pl.multiple_of(first_block * 128, 128), WIDE)

    copies = {}
    for i, (name, src, dst) in enumerate(
        [
            ("tokens", tokens_h, tokens),
            ("attn_gain", attn_gain_h, attn_gain),
            ("w_query", w_query_h, w_query),
            ("w_key", w_key_h.at[:, columns], w_key),
            ("w_value", w_value_h.at[:, columns], w_value),
            ("suf_keys", suffix_keys_h.at[:, :, columns], suf_keys),
            ("suf_values", suffix_values_h.at[:, :, columns], suf_values),
            ("w_out", w_out_h, w_out),
            ("mlp_gain", mlp_gain_h, mlp_gain),
            ("w_gate", w_gate_h, w_gate),
            ("w_up", w_up_h, w_up),
            ("w_down", w_down_h, w_down),
        ]
    ):
        copies[name] = pltpu.make_async_copy(src, dst, local_sem.at[i])
    key_copies = [
        pltpu.make_async_copy(prefix_keys_h.at[g, :, columns], keys.at[g], group_sem.at[0, g])
        for g in range(groups)
    ]
    value_copies = [
        pltpu.make_async_copy(prefix_values_h.at[g, :, columns], values.at[g], group_sem.at[1, g])
        for g in range(groups)
    ]
    for name in ("tokens", "attn_gain", "w_query", "w_key", "w_value", "suf_keys", "suf_values"):
        copies[name].start()
    for g in range(groups):
        key_copies[g].start()
        value_copies[g].start()
    for name in ("w_out", "mlp_gain", "w_gate", "w_up", "w_down"):
        copies[name].start()

    own_start = seq * rows
    own_group = column(group_of, own_start, rows)
    own_suffix = column(suffix_len, own_start, rows)
    own_prefix = jnp.zeros((rows, 1), jnp.int32)
    for g in range(groups):
        own_prefix = jnp.where(own_group == g, prefix_len[g], own_prefix)
    position = (own_prefix + own_suffix).astype(F32)
    turn = lane_ids((rows, 128)) % (HD // 2)
    frequency = jnp.ones((rows, 128), F32)
    for bit in range(5):
        step = 10000.0 ** (-(2**bit) / 32.0)
        frequency = jnp.where((turn // 2**bit) % 2 == 1, frequency * step, frequency)
    angles = position * frequency
    cosine, sine = jnp.cos(angles), jnp.sin(angles)
    cos2 = jnp.concatenate([cosine, cosine], axis=1)
    sin2 = jnp.concatenate([sine, sine], axis=1)
    cos3 = jnp.concatenate([cos2, cosine], axis=1)
    sin3 = jnp.concatenate([sin2, sine], axis=1)

    copies["tokens"].wait()
    copies["attn_gain"].wait()
    normed = rms(tokens[...], attn_gain[...].reshape(1, tokens.shape[1]))
    copies["w_query"].wait()
    q = dot_t(normed, w_query[...])
    q = jnp.concatenate([q, jnp.zeros((rows, PACK - q.shape[1]), F32)], axis=1)
    q_own = rotate(q, cos3, sin3).astype(BF16)
    queries[seq] = q_own
    pl.semaphore_wait(barrier, n_seq - 1 + n_tp - 1)

    def seq_copy(src, dst, send, recv, k):
        return pltpu.make_async_remote_copy(
            src_ref=src,
            dst_ref=dst,
            send_sem=send.at[k],
            recv_sem=recv.at[seq],
            device_id={"seq": lax.rem(seq + k, n_seq)},
            device_id_type=MESH,
        )

    def seq_wait(buf, send, recv, k):
        other = lax.rem(seq + k, n_seq)
        return pltpu.make_async_remote_copy(
            src_ref=buf.at[other],
            dst_ref=buf.at[other],
            send_sem=send.at[k],
            recv_sem=recv.at[other],
            device_id={"seq": other},
            device_id_type=MESH,
        )

    def over_peers(act):
        if n_seq <= 8:
            for k in range(1, n_seq):
                act(k)
        else:

            def step(k, carry):
                act(k)
                return carry

            lax.fori_loop(1, n_seq, step, 0)

    over_peers(
        lambda k: seq_copy(queries.at[seq], queries.at[seq], q_send, q_recv, k).start()
    )

    copies["w_key"].wait()
    copies["w_value"].wait()
    new_keys = rotate(dot(normed, w_key[...]), cos2, sin2).astype(BF16).astype(F32)
    new_values = dot(normed, w_value[...]).astype(BF16).astype(F32)
    q_wide = spread(q_own.astype(F32) * HD ** (-0.5), local_kv)
    own_score = jnp.sum(q_wide * jnp.concatenate([new_keys] * 5, axis=0), axis=1, keepdims=True)
    copies["suf_keys"].wait()
    suf_all = suf_keys[...].reshape(rows * suffix_span, WIDE)
    suf_scores = dot_t(q_wide.astype(BF16), suf_all)
    shape = suf_scores.shape
    spot = lane_ids(shape)
    row_id = lax.broadcasted_iota(jnp.int32, shape, 0) % rows
    limit = jnp.concatenate([own_suffix] * 5, axis=0)
    suf_live = (spot >= row_id * suffix_span) & (spot < row_id * suffix_span + limit)
    suf_scores = jnp.where(suf_live, suf_scores, NEG)
    suf_top = jnp.maximum(jnp.max(suf_scores, axis=1, keepdims=True), own_score)
    suf_weights = jnp.exp(suf_scores - suf_top)
    own_weight = jnp.exp(own_score - suf_top)
    suf_total = jnp.sum(suf_weights, axis=1, keepdims=True) + own_weight
    copies["suf_values"].wait()
    suf_mixed = dot(suf_weights.astype(BF16), suf_values[...].reshape(rows * suffix_span, WIDE))
    own_low = own_weight.astype(BF16).astype(F32)
    suf_mixed = suf_mixed + own_low * jnp.concatenate([new_values] * 5, axis=0)
    suf_blocks, suf_end, suf_sum = pack(suf_mixed, suf_top, suf_total, local_kv, rows)

    over_peers(lambda k: seq_wait(queries, q_send, q_recv, k).wait_recv())
    for g in range(groups):
        key_copies[g].wait()
        value_copies[g].wait()

    per_chunk = min(8, n_seq)
    chunk_rows = per_chunk * rows
    spots = seq * span + lane_ids((1, span))

    def prefix_chunk(c, carry):
        q_all = queries[pl.ds(c * per_chunk, per_chunk)].astype(F32).reshape(chunk_rows, PACK)
        q_all = spread(q_all * HD ** (-0.5), local_kv).astype(BF16)
        group = column(group_of, c * chunk_rows, chunk_rows)
        group = jnp.concatenate([group] * 5, axis=0)
        mixed = jnp.zeros((5 * chunk_rows, WIDE), F32)
        tops = jnp.full((5 * chunk_rows, 1), NEG, F32)
        sums = jnp.zeros((5 * chunk_rows, 128), F32)
        for g in range(groups):
            scores = jnp.where(spots < prefix_len[g], dot_t(q_all, keys[g]), NEG)
            top = jnp.max(fold_max(scores), axis=1, keepdims=True)
            member = group == g
            tops = jnp.where(member, top, tops)
            weights = jnp.exp(scores - jnp.where(member, top, -NEG))
            sums += fold_lanes(weights)
            mixed += dot(weights.astype(BF16), values[g])
        totals = jnp.sum(sums, axis=1, keepdims=True)
        blocks, top_row, total_row = pack(mixed, tops, totals, local_kv, chunk_rows)
        for i, term in enumerate(terms(top_row) + terms(total_row)):
            blocks[2] = blocks[2] + (term if i == 0 else pltpu.roll(term, 8 * i, 1))
        packed = jnp.concatenate(blocks, axis=1).reshape(per_chunk, rows, PACK)
        send_parts[pl.ds(c * per_chunk, per_chunk)] = packed.astype(BF16)
        return carry

    if n_seq == per_chunk:
        prefix_chunk(0, 0)
    else:
        lax.fori_loop(0, n_seq // per_chunk, prefix_chunk, 0)

    def send_part(k):
        other = lax.rem(seq + k, n_seq)
        seq_copy(send_parts.at[other], parts.at[seq], p_send, p_recv, k).start()

    over_peers(send_part)
    parts[seq] = send_parts[seq]
    over_peers(lambda k: seq_wait(parts, p_send, p_recv, k).wait_recv())

    every = parts[...].astype(F32)
    ends = every[:, :, 256:].reshape(n_seq * rows, 128)
    rolled = [ends] + [pltpu.roll(ends, 128 - 8 * i, 1) for i in range(1, 6)]
    part_tops = (rolled[0] + rolled[1] + rolled[2]).reshape(n_seq, rows, 128)
    part_sums = (rolled[3] + rolled[4] + rolled[5]).reshape(n_seq, rows, 128)
    top = jnp.maximum(jnp.max(part_tops, axis=0), suf_end)
    scales = jnp.exp(part_tops - top[None])
    suf_scale = jnp.exp(suf_end - top)
    total = suf_scale * suf_sum + jnp.sum(scales * part_sums, axis=0)
    used_lane = lane_ids((rows, 128)) - HD < used
    share_of = jnp.where(used_lane, 1.0 / total, 0.0)
    half = lane_ids((rows, 128)) < HD

    def weigh(scale, part):
        scale = scale * share_of
        cols = [scale[:, HD + s : HD + s + 1] for s in range(5)]
        return jnp.concatenate(
            [
                jnp.where(half, cols[0], cols[1]) * part[:, :128],
                jnp.where(half, cols[2], cols[3]) * part[:, 128:256],
                jnp.where(half, cols[4], 0.0) * part[:, 256:],
            ],
            axis=1,
        )

    attended = weigh(suf_scale, jnp.concatenate(suf_blocks, axis=1))
    for i in range(n_seq):
        attended = attended + weigh(scales[i], every[i])
    attended = attended[:, : 5 * HD].astype(BF16)

    def tp_sum(buf, send, recv):
        for k in range(1, n_tp):
            pltpu.make_async_remote_copy(
                src_ref=buf.at[tp],
                dst_ref=buf.at[tp],
                send_sem=send.at[k],
                recv_sem=recv.at[tp],
                device_id={"tp": lax.rem(tp + k, n_tp)},
                device_id_type=MESH,
            ).start()
        for k in range(1, n_tp):
            other = lax.rem(tp + k, n_tp)
            pltpu.make_async_remote_copy(
                src_ref=buf.at[other],
                dst_ref=buf.at[other],
                send_sem=send.at[k],
                recv_sem=recv.at[other],
                device_id={"tp": other},
                device_id_type=MESH,
            ).wait_recv()
        total = buf[0].astype(F32)
        for i in range(1, n_tp):
            total = total + buf[i].astype(F32)
        return total

    copies["w_out"].wait()
    head_parts[tp] = dot(attended, w_out[...]).astype(BF16)
    hidden = (tokens[...].astype(F32) + tp_sum(head_parts, h_send, h_recv)).astype(BF16)
    copies["mlp_gain"].wait()
    mlp_in = rms(hidden, mlp_gain[...].reshape(1, tokens.shape[1]))
    copies["w_gate"].wait()
    gate = dot(mlp_in, w_gate[...])
    copies["w_up"].wait()
    up = dot(mlp_in, w_up[...])
    activation = (gate / (1.0 + jnp.exp(-gate)) * up).astype(BF16)
    copies["w_down"].wait()
    down_parts[tp] = dot(activation, w_down[...]).astype(BF16)
    total = tp_sum(down_parts, d_send, d_recv)
    out_ref[...] = (hidden.astype(F32) + total).astype(BF16)

    over_peers(
        lambda k: seq_copy(queries.at[seq], queries.at[seq], q_send, q_recv, k).wait_send()
    )

    def sent_part(k):
        other = lax.rem(seq + k, n_seq)
        seq_copy(send_parts.at[other], parts.at[seq], p_send, p_recv, k).wait_send()

    over_peers(sent_part)
    for buf, send, recv in ((head_parts, h_send, h_recv), (down_parts, d_send, d_recv)):
        for k in range(1, n_tp):
            pltpu.make_async_remote_copy(
                src_ref=buf.at[tp],
                dst_ref=buf.at[tp],
                send_sem=send.at[k],
                recv_sem=recv.at[tp],
                device_id={"tp": lax.rem(tp + k, n_tp)},
                device_id_type=MESH,
            ).wait_send()


def on_device(n_seq, n_tp, *args):
    tokens, w_query, w_out, w_gate, w_down = args[0], args[2], args[5], args[14], args[16]
    prefix, suffix = args[6], args[8]
    rows, width = tokens.shape
    groups, span, _ = prefix.shape
    hidden_units = w_gate.shape[1]
    dma = pltpu.SemaphoreType.DMA
    args = list(args)
    args[2] = w_query.T
    in_specs = [pl.BlockSpec(memory_space=pl.ANY)] * len(args)
    for i in (10, 11, 12):
        in_specs[i] = pl.BlockSpec(memory_space=pltpu.SMEM)
    return pl.pallas_call(
        functools.partial(kernel, n_seq, n_tp),
        out_shape=jax.ShapeDtypeStruct((rows, width), BF16),
        in_specs=in_specs,
        out_specs=pl.BlockSpec(memory_space=pltpu.VMEM),
        scratch_shapes=[
            pltpu.VMEM((rows, width), BF16),
            pltpu.VMEM((width,), F32),
            pltpu.VMEM(w_query.shape[::-1], BF16),
            pltpu.VMEM((width, WIDE), BF16),
            pltpu.VMEM((width, WIDE), BF16),
            pltpu.VMEM(w_out.shape, BF16),
            pltpu.VMEM((groups, span, WIDE), BF16),
            pltpu.VMEM((groups, span, WIDE), BF16),
            pltpu.VMEM((rows, suffix.shape[1], WIDE), BF16),
            pltpu.VMEM((rows, suffix.shape[1], WIDE), BF16),
            pltpu.VMEM((width,), F32),
            pltpu.VMEM(w_gate.shape, BF16),
            pltpu.VMEM(w_gate.shape, BF16),
            pltpu.VMEM(w_down.shape, BF16),
            pltpu.VMEM((n_seq, rows, PACK), BF16),
            pltpu.VMEM((n_seq, rows, PACK), BF16),
            pltpu.VMEM((n_seq, rows, PACK), BF16),
            pltpu.VMEM((n_tp, rows, width), BF16),
            pltpu.VMEM((n_tp, rows, width), BF16),
            dma((12,)),
            dma((2, groups)),
            dma((n_seq,)),
            dma((n_seq,)),
            dma((n_seq,)),
            dma((n_seq,)),
            dma((n_tp,)),
            dma((n_tp,)),
            dma((n_tp,)),
            dma((n_tp,)),
        ],
        compiler_params=pltpu.CompilerParams(
            collective_id=0, has_side_effects=True, vmem_limit_bytes=56 * 1024 * 1024
        ),
    )(*args)


def solution(mesh):
    return jax.shard_map(
        functools.partial(on_device, mesh.shape["seq"], mesh.shape["tp"]),
        mesh=mesh,
        in_specs=(
            P("seq", None),
            P(),
            P(None, "tp"),
            P(),
            P(),
            P("tp", None),
            P(None, "seq", None),
            P(None, "seq", None),
            P("seq", None, None),
            P("seq", None, None),
            P(),
            P(),
            P(),
            P(),
            P(None, "tp"),
            P(None, "tp"),
            P("tp", None),
        ),
        out_specs=P("seq", None),
        check_vma=False,
    )
```

```python
import functools

import jax
import jax.numpy as jnp
from jax import lax
from jax.experimental import pallas as pl
from jax.experimental.pallas import tpu as pltpu
from jax.sharding import PartitionSpec as P

HEADS = 18
KV_HEADS = 6
HD = 64
NEG = -1e30
WIDE = 256
PACK = 384
MESH = pl.DeviceIdType.MESH
F32 = jnp.float32
BF16 = jnp.bfloat16


def lane_ids(shape):
    return lax.broadcasted_iota(jnp.int32, shape, len(shape) - 1)


def rms(values, gain):
    wide = values.astype(F32)
    factor = lax.rsqrt(jnp.mean(wide * wide, axis=-1, keepdims=True) + 1e-05)
    return (wide * factor * gain).astype(BF16)


def dot(a, b):
    return jnp.dot(a, b, preferred_element_type=F32)


def dot_t(a, b):
    return lax.dot_general(a, b, (((1,), (1,)), ((), ())), preferred_element_type=F32)


def rotate(x, cosine, sine):
    width = x.shape[-1]
    low = lane_ids(x.shape) % HD < HD // 2
    ahead = pltpu.roll(x, width - HD // 2, 1)
    behind = pltpu.roll(x, HD // 2, 1)
    return x * cosine + jnp.where(low, -ahead, behind) * sine


def spread(q, local_kv):
    rows = q.shape[0]
    half = lane_ids((rows, 128)) < HD
    quarter = lane_ids((rows, WIDE)) // HD
    blocks = []
    for s, kv in enumerate(local_kv):
        pair = q[:, 128 * (s // 2) : 128 * (s // 2) + 128]
        turned = pltpu.roll(pair, HD, 1)
        both = jnp.where(half, pair, turned) if s % 2 == 0 else jnp.where(half, turned, pair)
        wide = jnp.concatenate([both, both], axis=1)
        blocks.append(jnp.where(quarter == kv, wide, 0.0))
    return jnp.concatenate(blocks, axis=0)


def pack(mixed, tops, totals, local_kv, rows):
    lanes = lane_ids((rows, 128))
    quarter = lane_ids((rows, WIDE)) // HD
    both = []
    for s, kv in enumerate(local_kv):
        part = jnp.where(quarter == kv, mixed[s * rows : (s + 1) * rows], 0.0)
        part = part[:, :128] + part[:, 128:]
        both.append(part + pltpu.roll(part, HD, 1))
    top_row = jnp.zeros((rows, 128), F32)
    total_row = jnp.zeros((rows, 128), F32)
    for s in range(5):
        top_row = jnp.where(lanes == HD + s, tops[s * rows : (s + 1) * rows], top_row)
        total_row = jnp.where(lanes == HD + s, totals[s * rows : (s + 1) * rows], total_row)
    blocks = [
        jnp.where(lanes < HD, both[0], both[1]),
        jnp.where(lanes < HD, both[2], both[3]),
        jnp.where(lanes < HD, both[4], 0.0),
    ]
    return blocks, top_row, total_row


def terms(x):
    high = x.astype(BF16).astype(F32)
    middle = (x - high).astype(BF16).astype(F32)
    return high, middle, x - high - middle


def fold_lanes(x):
    out = x[:, :128]
    for i in range(128, x.shape[1], 128):
        out = out + x[:, i : i + 128]
    return out


def fold_max(x):
    out = x[:, :128]
    for i in range(128, x.shape[1], 128):
        out = jnp.maximum(out, x[:, i : i + 128])
    return out


def column(ref, start, rows):
    ids = lax.broadcasted_iota(jnp.int32, (8, 1), 0)
    blocks = []
    for block in range(rows // 8):
        col = jnp.zeros((8, 1), jnp.int32)
        for r in range(8):
            col = jnp.where(ids == r, ref[start + block * 8 + r], col)
        blocks.append(col)
    return blocks[0] if len(blocks) == 1 else jnp.concatenate(blocks, axis=0)


def kernel(
    n_seq,
    n_tp,
    tokens_h,
    attn_gain_h,
    w_query_h,
    w_key_h,
    w_value_h,
    w_out_h,
    prefix_keys_h,
    prefix_values_h,
    suffix_keys_h,
    suffix_values_h,
    group_of,
    prefix_len,
    suffix_len,
    mlp_gain_h,
    w_gate_h,
    w_up_h,
    w_down_h,
    out_ref,
    tokens,
    attn_gain,
    w_query,
    w_key,
    w_value,
    w_out,
    keys,
    values,
    suf_keys,
    suf_values,
    mlp_gain,
    w_gate,
    w_up,
    w_down,
    queries,
    send_parts,
    parts,
    head_parts,
    down_parts,
    local_sem,
    group_sem,
    q_send,
    q_recv,
    p_send,
    p_recv,
    h_send,
    h_recv,
    d_send,
    d_recv,
):
    seq = lax.axis_index("seq")
    tp = lax.axis_index("tp")
    rows = tokens.shape[0]
    groups, span = keys.shape[0], keys.shape[1]
    suffix_span = suf_keys.shape[1]

    barrier = pltpu.get_barrier_semaphore()

    def greet(k, carry):
        pl.semaphore_signal(
            barrier, inc=1, device_id={"seq": lax.rem(seq + k, n_seq)}, device_id_type=MESH
        )
        return carry

    if n_seq <= 8:
        for k in range(1, n_seq):
            greet(k, 0)
    else:
        lax.fori_loop(1, n_seq, greet, 0)
    for k in range(1, n_tp):
        pl.semaphore_signal(
            barrier, inc=1, device_id={"tp": lax.rem(tp + k, n_tp)}, device_id_type=MESH
        )

    per, surplus = HEADS // n_tp, HEADS % n_tp
    first_head = per * tp + jnp.minimum(tp, surplus)
    used = per + (tp < surplus).astype(jnp.int32)
    share = HEADS // KV_HEADS
    first_block = jnp.minimum((first_head // share) // 2, 1)
    local_kv = [
        jnp.minimum(first_head + s, HEADS - 1) // share - 2 * first_block for s in range(5)
    ]
    columns = pl.ds(pl.multiple_of(first_block * 128, 128), WIDE)

    copies = {}
    for i, (name, src, dst) in enumerate(
        [
            ("tokens", tokens_h, tokens),
            ("attn_gain", attn_gain_h, attn_gain),
            ("w_query", w_query_h, w_query),
            ("w_key", w_key_h.at[:, columns], w_key),
            ("w_value", w_value_h.at[:, columns], w_value),
            ("suf_keys", suffix_keys_h.at[:, :, columns], suf_keys),
            ("suf_values", suffix_values_h.at[:, :, columns], suf_values),
            ("w_out", w_out_h, w_out),
            ("mlp_gain", mlp_gain_h, mlp_gain),
            ("w_gate", w_gate_h, w_gate),
            ("w_up", w_up_h, w_up),
            ("w_down", w_down_h, w_down),
        ]
    ):
        copies[name] = pltpu.make_async_copy(src, dst, local_sem.at[i])
    key_copies = [
        pltpu.make_async_copy(prefix_keys_h.at[g, :, columns], keys.at[g], group_sem.at[0, g])
        for g in range(groups)
    ]
    value_copies = [
        pltpu.make_async_copy(prefix_values_h.at[g, :, columns], values.at[g], group_sem.at[1, g])
        for g in range(groups)
    ]
    for name in ("tokens", "attn_gain", "w_query", "w_key", "w_value", "suf_keys", "suf_values"):
        copies[name].start()
    for g in range(groups):
        key_copies[g].start()
        value_copies[g].start()
    for name in ("w_out", "mlp_gain", "w_gate", "w_up", "w_down"):
        copies[name].start()

    own_start = seq * rows
    own_group = column(group_of, own_start, rows)
    own_suffix = column(suffix_len, own_start, rows)
    own_prefix = jnp.zeros((rows, 1), jnp.int32)
    for g in range(groups):
        own_prefix = jnp.where(own_group == g, prefix_len[g], own_prefix)
    position = (own_prefix + own_suffix).astype(F32)
    turn = lane_ids((rows, 128)) % (HD // 2)
    frequency = jnp.ones((rows, 128), F32)
    for bit in range(5):
        step = 10000.0 ** (-(2**bit) / 32.0)
        frequency = jnp.where((turn // 2**bit) % 2 == 1, frequency * step, frequency)
    angles = position * frequency
    cosine, sine = jnp.cos(angles), jnp.sin(angles)
    cos2 = jnp.concatenate([cosine, cosine], axis=1)
    sin2 = jnp.concatenate([sine, sine], axis=1)
    cos3 = jnp.concatenate([cos2, cosine], axis=1)
    sin3 = jnp.concatenate([sin2, sine], axis=1)

    copies["tokens"].wait()
    copies["attn_gain"].wait()
    normed = rms(tokens[...], attn_gain[...].reshape(1, tokens.shape[1]))
    copies["w_query"].wait()
    q = dot_t(normed, w_query[...])
    q = jnp.concatenate([q, jnp.zeros((rows, PACK - q.shape[1]), F32)], axis=1)
    q_own = rotate(q, cos3, sin3).astype(BF16)
    queries[seq] = q_own
    pl.semaphore_wait(barrier, n_seq - 1 + n_tp - 1)

    def seq_copy(src, dst, send, recv, k):
        return pltpu.make_async_remote_copy(
            src_ref=src,
            dst_ref=dst,
            send_sem=send.at[k],
            recv_sem=recv.at[seq],
            device_id={"seq": lax.rem(seq + k, n_seq)},
            device_id_type=MESH,
        )

    def seq_wait(buf, send, recv, k):
        other = lax.rem(seq + k, n_seq)
        return pltpu.make_async_remote_copy(
            src_ref=buf.at[other],
            dst_ref=buf.at[other],
            send_sem=send.at[k],
            recv_sem=recv.at[other],
            device_id={"seq": other},
            device_id_type=MESH,
        )

    def over_peers(act):
        if n_seq <= 8:
            for k in range(1, n_seq):
                act(k)
        else:

            def step(k, carry):
                act(k)
                return carry

            lax.fori_loop(1, n_seq, step, 0)

    over_peers(
        lambda k: seq_copy(queries.at[seq], queries.at[seq], q_send, q_recv, k).start()
    )

    copies["w_key"].wait()
    copies["w_value"].wait()
    new_keys = rotate(dot(normed, w_key[...]), cos2, sin2).astype(BF16).astype(F32)
    new_values = dot(normed, w_value[...]).astype(BF16).astype(F32)
    q_wide = spread(q_own.astype(F32) * HD ** (-0.5), local_kv)
    own_score = jnp.sum(q_wide * jnp.concatenate([new_keys] * 5, axis=0), axis=1, keepdims=True)
    copies["suf_keys"].wait()
    suf_all = suf_keys[...].reshape(rows * suffix_span, WIDE)
    suf_scores = dot_t(q_wide.astype(BF16), suf_all)
    shape = suf_scores.shape
    spot = lane_ids(shape)
    row_id = lax.broadcasted_iota(jnp.int32, shape, 0) % rows
    limit = jnp.concatenate([own_suffix] * 5, axis=0)
    suf_live = (spot >= row_id * suffix_span) & (spot < row_id * suffix_span + limit)
    suf_scores = jnp.where(suf_live, suf_scores, NEG)
    suf_top = jnp.maximum(jnp.max(suf_scores, axis=1, keepdims=True), own_score)
    suf_weights = jnp.exp(suf_scores - suf_top)
    own_weight = jnp.exp(own_score - suf_top)
    suf_total = jnp.sum(suf_weights, axis=1, keepdims=True) + own_weight
    copies["suf_values"].wait()
    suf_mixed = dot(suf_weights.astype(BF16), suf_values[...].reshape(rows * suffix_span, WIDE))
    own_low = own_weight.astype(BF16).astype(F32)
    suf_mixed = suf_mixed + own_low * jnp.concatenate([new_values] * 5, axis=0)
    suf_blocks, suf_end, suf_sum = pack(suf_mixed, suf_top, suf_total, local_kv, rows)

    over_peers(lambda k: seq_wait(queries, q_send, q_recv, k).wait_recv())
    for g in range(groups):
        key_copies[g].wait()
        value_copies[g].wait()

    per_chunk = min(8, n_seq)
    chunk_rows = per_chunk * rows
    spots = seq * span + lane_ids((1, span))

    def prefix_chunk(c, carry):
        q_all = queries[pl.ds(c * per_chunk, per_chunk)].astype(F32).reshape(chunk_rows, PACK)
        q_all = spread(q_all * HD ** (-0.5), local_kv).astype(BF16)
        group = column(group_of, c * chunk_rows, chunk_rows)
        group = jnp.concatenate([group] * 5, axis=0)
        mixed = jnp.zeros((5 * chunk_rows, WIDE), F32)
        tops = jnp.full((5 * chunk_rows, 1), NEG, F32)
        sums = jnp.zeros((5 * chunk_rows, 128), F32)
        for g in range(groups):
            scores = jnp.where(spots < prefix_len[g], dot_t(q_all, keys[g]), NEG)
            top = jnp.max(fold_max(scores), axis=1, keepdims=True)
            member = group == g
            tops = jnp.where(member, top, tops)
            weights = jnp.exp(scores - jnp.where(member, top, -NEG))
            sums += fold_lanes(weights)
            mixed += dot(weights.astype(BF16), values[g])
        totals = jnp.sum(sums, axis=1, keepdims=True)
        blocks, top_row, total_row = pack(mixed, tops, totals, local_kv, chunk_rows)
        for i, term in enumerate(terms(top_row) + terms(total_row)):
            blocks[2] = blocks[2] + (term if i == 0 else pltpu.roll(term, 8 * i, 1))
        packed = jnp.concatenate(blocks, axis=1).reshape(per_chunk, rows, PACK)
        send_parts[pl.ds(c * per_chunk, per_chunk)] = packed.astype(BF16)
        return carry

    if n_seq == per_chunk:
        prefix_chunk(0, 0)
    else:
        lax.fori_loop(0, n_seq // per_chunk, prefix_chunk, 0)

    def send_part(k):
        other = lax.rem(seq + k, n_seq)
        seq_copy(send_parts.at[other], parts.at[seq], p_send, p_recv, k).start()

    over_peers(send_part)
    parts[seq] = send_parts[seq]
    over_peers(lambda k: seq_wait(parts, p_send, p_recv, k).wait_recv())

    every = parts[...].astype(F32)
    ends = every[:, :, 256:].reshape(n_seq * rows, 128)
    rolled = [ends] + [pltpu.roll(ends, 128 - 8 * i, 1) for i in range(1, 6)]
    part_tops = (rolled[0] + rolled[1] + rolled[2]).reshape(n_seq, rows, 128)
    part_sums = (rolled[3] + rolled[4] + rolled[5]).reshape(n_seq, rows, 128)
    top = jnp.maximum(jnp.max(part_tops, axis=0), suf_end)
    scales = jnp.exp(part_tops - top[None])
    suf_scale = jnp.exp(suf_end - top)
    total = suf_scale * suf_sum + jnp.sum(scales * part_sums, axis=0)
    used_lane = lane_ids((rows, 128)) - HD < used
    share_of = jnp.where(used_lane, 1.0 / total, 0.0)
    half = lane_ids((rows, 128)) < HD

    def weigh(scale, part):
        scale = scale * share_of
        cols = [scale[:, HD + s : HD + s + 1] for s in range(5)]
        return jnp.concatenate(
            [
                jnp.where(half, cols[0], cols[1]) * part[:, :128],
                jnp.where(half, cols[2], cols[3]) * part[:, 128:256],
                jnp.where(half, cols[4], 0.0) * part[:, 256:],
            ],
            axis=1,
        )

    attended = weigh(suf_scale, jnp.concatenate(suf_blocks, axis=1))
    for i in range(n_seq):
        attended = attended + weigh(scales[i], every[i])
    attended = attended[:, : 5 * HD].astype(BF16)

    width = tokens.shape[1]
    cut = 512 if width > 512 else width
    pieces = [(0, cut)] + ([(cut, width - cut)] if width > cut else [])

    def tp_copy(buf, send, recv, k, c, owner):
        piece = buf.at[owner, :, pl.ds(*pieces[c])]
        return pltpu.make_async_remote_copy(
            src_ref=piece,
            dst_ref=piece,
            send_sem=send.at[c, k],
            recv_sem=recv.at[c, owner],
            device_id={"tp": lax.rem(tp + k, n_tp)},
            device_id_type=MESH,
        )

    def tp_sum(left, weight, buf, send, recv):
        for c, (start, size) in enumerate(pieces):
            piece = dot(left, weight[:, start : start + size]).astype(BF16)
            buf[tp, :, start : start + size] = piece
            for k in range(1, n_tp):
                tp_copy(buf, send, recv, k, c, tp).start()
        for c in range(len(pieces)):
            for k in range(1, n_tp):
                tp_copy(buf, send, recv, k, c, lax.rem(tp + k, n_tp)).wait_recv()
        total = buf[0].astype(F32)
        for i in range(1, n_tp):
            total = total + buf[i].astype(F32)
        return total

    copies["w_out"].wait()
    total = tp_sum(attended, w_out, head_parts, h_send, h_recv)
    hidden = (tokens[...].astype(F32) + total).astype(BF16)
    copies["mlp_gain"].wait()
    mlp_in = rms(hidden, mlp_gain[...].reshape(1, tokens.shape[1]))
    copies["w_gate"].wait()
    gate = dot(mlp_in, w_gate[...])
    copies["w_up"].wait()
    up = dot(mlp_in, w_up[...])
    activation = (gate / (1.0 + jnp.exp(-gate)) * up).astype(BF16)
    copies["w_down"].wait()
    total = tp_sum(activation, w_down, down_parts, d_send, d_recv)
    out_ref[...] = (hidden.astype(F32) + total).astype(BF16)

    over_peers(
        lambda k: seq_copy(queries.at[seq], queries.at[seq], q_send, q_recv, k).wait_send()
    )

    def sent_part(k):
        other = lax.rem(seq + k, n_seq)
        seq_copy(send_parts.at[other], parts.at[seq], p_send, p_recv, k).wait_send()

    over_peers(sent_part)
    for buf, send, recv in ((head_parts, h_send, h_recv), (down_parts, d_send, d_recv)):
        for c in range(len(pieces)):
            for k in range(1, n_tp):
                tp_copy(buf, send, recv, k, c, tp).wait_send()


def on_device(n_seq, n_tp, *args):
    tokens, w_query, w_out, w_gate, w_down = args[0], args[2], args[5], args[14], args[16]
    prefix, suffix = args[6], args[8]
    rows, width = tokens.shape
    groups, span, _ = prefix.shape
    hidden_units = w_gate.shape[1]
    dma = pltpu.SemaphoreType.DMA
    args = list(args)
    args[2] = w_query.T
    in_specs = [pl.BlockSpec(memory_space=pl.ANY)] * len(args)
    for i in (10, 11, 12):
        in_specs[i] = pl.BlockSpec(memory_space=pltpu.SMEM)
    return pl.pallas_call(
        functools.partial(kernel, n_seq, n_tp),
        out_shape=jax.ShapeDtypeStruct((rows, width), BF16),
        in_specs=in_specs,
        out_specs=pl.BlockSpec(memory_space=pltpu.VMEM),
        scratch_shapes=[
            pltpu.VMEM((rows, width), BF16),
            pltpu.VMEM((width,), F32),
            pltpu.VMEM(w_query.shape[::-1], BF16),
            pltpu.VMEM((width, WIDE), BF16),
            pltpu.VMEM((width, WIDE), BF16),
            pltpu.VMEM(w_out.shape, BF16),
            pltpu.VMEM((groups, span, WIDE), BF16),
            pltpu.VMEM((groups, span, WIDE), BF16),
            pltpu.VMEM((rows, suffix.shape[1], WIDE), BF16),
            pltpu.VMEM((rows, suffix.shape[1], WIDE), BF16),
            pltpu.VMEM((width,), F32),
            pltpu.VMEM(w_gate.shape, BF16),
            pltpu.VMEM(w_gate.shape, BF16),
            pltpu.VMEM(w_down.shape, BF16),
            pltpu.VMEM((n_seq, rows, PACK), BF16),
            pltpu.VMEM((n_seq, rows, PACK), BF16),
            pltpu.VMEM((n_seq, rows, PACK), BF16),
            pltpu.VMEM((n_tp, rows, width), BF16),
            pltpu.VMEM((n_tp, rows, width), BF16),
            dma((12,)),
            dma((2, groups)),
            dma((n_seq,)),
            dma((n_seq,)),
            dma((n_seq,)),
            dma((n_seq,)),
            dma((2, n_tp)),
            dma((2, n_tp)),
            dma((2, n_tp)),
            dma((2, n_tp)),
        ],
        compiler_params=pltpu.CompilerParams(
            collective_id=0, has_side_effects=True, vmem_limit_bytes=56 * 1024 * 1024
        ),
    )(*args)


def solution(mesh):
    return jax.shard_map(
        functools.partial(on_device, mesh.shape["seq"], mesh.shape["tp"]),
        mesh=mesh,
        in_specs=(
            P("seq", None),
            P(),
            P(None, "tp"),
            P(),
            P(),
            P("tp", None),
            P(None, "seq", None),
            P(None, "seq", None),
            P("seq", None, None),
            P("seq", None, None),
            P(),
            P(),
            P(),
            P(),
            P(None, "tp"),
            P(None, "tp"),
            P("tp", None),
        ),
        out_specs=P("seq", None),
        check_vma=False,
    )
```
